32 devices in a mesh: grp: 8 (over z, core), tp: 4 (over y, x).
Axes of the slice: x: 2, y: 2, z: 4, core: 2. Of those that a mesh axis runs over, the one named last changes fastest.
Arguments:
- query_heads: bfloat16 [4096, 4096], P('grp', 'tp'), may hold values from -6 to 6
- key_heads: bfloat16 [4096, 4096], P('grp', 'tp'), may hold values from -6 to 6
- value_heads: bfloat16 [4096, 4096], P('grp', 'tp'), may hold values from -12 to 12
- modality: int32 [8, 768], P('grp'), may hold values from 0 to 1, as said below
- doc_ids: int32 [8, 768], P('grp'), may hold values from 0 to 188, as said below
- out_weight: bfloat16 [2, 4096, 4096], P(None, 'tp'), may hold values from -0.1875 to 0.1875
- out_grad: bfloat16 [4096, 4096], P('grp'), may hold values from -6 to 6
Outputs:
- layer_output: bfloat16 [4096, 4096], P('grp', 'tp')
- grad_query: bfloat16 [4096, 4096], P('grp', 'tp')
- grad_key: bfloat16 [4096, 4096], P('grp', 'tp')
- grad_value: bfloat16 [4096, 4096], P('grp', 'tp')
The draws below stay inside these ranges and needn't reach their ends.
Inputs may be any that keep to these rules, and one draw needn't show every extreme that they name: `modality`: row g and row g + 4 describe the same pack. 0 marks a text position, 1 an image position. Positions 0 to 15 alternate text, image. Every pack holds 256 to 512 text positions; some pack holds exactly 512 text positions and some exactly 512 image positions. `doc_ids`: row g and row g + 4 describe the same pack. The document number is 0 at position 0, never falls and rises by at most one a position; a new document starts only at positions of 16 or more that are multiples of 4.
All inputs are finite; a program needn't handle non-finite values.
Results may differ from the reference program's by a relative error of at most 0.028.
Values may be sent and summed in bfloat16 or wider, within the bound.
A program may use at most 128 MiB of HBM per device.

```python
import jax
import jax.numpy as jnp
from jax import lax

D = 4096
HEADS = 32
HD = 128
ROWS = 512
PACK = 768
INNER = 4096
ALLROWS = 4096
N_GRP = 8


def pack_layout(seed_key):
    base_key = jax.random.fold_in(seed_key, 7)
    pair_count = N_GRP // 2

    def one_pack(pack_index):
        pack_key = jax.random.fold_in(base_key, pack_index)
        count_key, order_key, start_key = jax.random.split(pack_key, 3)
        text_count = jax.random.randint(count_key, (), PACK - ROWS, ROWS + 1)
        text_count = jnp.where(pack_index == 0, ROWS, jnp.where(pack_index == 1, PACK - ROWS, text_count))
        shuffled = jax.random.permutation(order_key, PACK - 16)
        rest_modal = jnp.where(shuffled < text_count - 8, 0, 1).astype(jnp.int32)
        prefix = jnp.arange(16, dtype=jnp.int32) % 2
        modal_row = jnp.concatenate((prefix, rest_modal))
        spots = jnp.arange(PACK, dtype=jnp.int32)
        eligible = (spots >= 16) & (spots % 4 == 0)
        random_starts = jax.random.randint(start_key, (PACK,), 0, max(PACK // 16, 2)) == 0
        starts = eligible & (random_starts | (pack_index == 0))
        starts = starts | (spots == 0)
        doc_row = (jnp.cumsum(starts.astype(jnp.int32)) - 1).astype(jnp.int32)
        return (modal_row, doc_row)
    modal_rows, doc_rows = jax.vmap(one_pack)(jnp.arange(pair_count, dtype=jnp.int32))
    return (jnp.concatenate((modal_rows, modal_rows)), jnp.concatenate((doc_rows, doc_rows)))


def draw_modality(key, part):
    return pack_layout(key)[0]


def draw_doc_ids(key, part):
    return pack_layout(key)[1]


def draw_query_heads(key, part):
    shape = (N_GRP * ROWS, HEADS * HD)
    own_key = jax.random.fold_in(key, 1)
    result = jnp.clip(jax.random.normal(own_key, shape, jnp.float32), -4.0, 4.0)
    return result.astype(jnp.bfloat16)


def draw_key_heads(key, part):
    shape = (N_GRP * ROWS, HEADS * HD)
    own_key = jax.random.fold_in(key, 2)
    result = jnp.clip(jax.random.normal(own_key, shape, jnp.float32), -4.0, 4.0)
    return result.astype(jnp.bfloat16)


def levels(key, extent, cuts, least, top_value):
    def one(position, parts):
        draws = jax.random.uniform(jax.random.fold_in(jax.random.fold_in(key, 6), position), (parts,), jnp.float32, least / len(cuts), top_value / len(cuts))
        return jnp.repeat(jnp.exp(draws), extent[position] // parts).reshape((-1,) + (1,) * (len(extent) - position - 1))

    factor_of = one(*cuts[0])
    for cut in cuts[1:]:
        factor_of = factor_of * one(*cut)
    return factor_of


def gaussian(stream_key, shape, width, limit, pieces=(), kind=jnp.bfloat16):
    entries = width * jax.random.normal(stream_key, shape, jnp.float32)
    if pieces:
        entries = entries * levels(stream_key, shape, pieces, -0.22, 0.18)
    return jnp.clip(entries, -limit, limit).astype(kind)


def setup_inputs(seed: int = 0) -> dict:
    streams_of = jax.random.split(jax.random.key(seed), 8)
    query_heads = draw_query_heads(jax.random.fold_in(streams_of[7], 71), 0)
    key_heads = draw_key_heads(jax.random.fold_in(streams_of[7], 71), 0)
    value_heads = gaussian(streams_of[2], (ALLROWS, INNER), 2.0, 12.0, ((0, 8), (1, 4)))
    modality = draw_modality(jax.random.fold_in(streams_of[7], 71), 0)
    doc_ids = draw_doc_ids(jax.random.fold_in(streams_of[7], 71), 0)
    out_weight = gaussian(streams_of[5], (2, INNER, D), (INNER // 4) ** -0.5, 0.1875, ((1, 4),))
    out_grad = gaussian(streams_of[6], (ALLROWS, D), 1.0, 6.0, ((0, 8),))
    return {"query_heads": query_heads, "key_heads": key_heads, "value_heads": value_heads, "modality": modality, "doc_ids": doc_ids, "out_weight": out_weight, "out_grad": out_grad}


MASKED = -1.0e30


def rounded(array):
    return lax.optimization_barrier(array.astype(jnp.bfloat16)).astype(jnp.float32)


def slot_info(modal_row, doc_row, modal_side, row_count):
    pack_len = modal_row.shape[0]
    chosen = modal_row == modal_side
    slot_pos = jnp.nonzero(chosen, size=row_count, fill_value=pack_len - 1)[0].astype(jnp.int32)
    slot_doc = jnp.take(doc_row, slot_pos)
    live_slot = jnp.arange(row_count, dtype=jnp.int32) < jnp.sum(chosen.astype(jnp.int32))
    return slot_pos, slot_doc, live_slot


def allowed(query_info, key_info):
    before = key_info[0][None, :] <= query_info[0][:, None]
    same_doc = key_info[1][None, :] == query_info[1][:, None]
    return before & same_doc & key_info[2][None, :]


def pair_layer(packed):
    modal_row, doc_row, query_pair, key_pair, value_pair, grad_pair = packed
    row_count = query_pair.shape[1]
    text_info = slot_info(modal_row, doc_row, 0, row_count)
    image_info = slot_info(modal_row, doc_row, 1, row_count)
    joined = tuple(jnp.concatenate((text_part, image_part)) for text_part, image_part in zip(text_info, image_info))
    permit = allowed(joined, joined)
    shape3 = (2 * row_count, HEADS, HD)
    q_all = query_pair.reshape(shape3).astype(jnp.float32)
    k_all = key_pair.reshape(shape3).astype(jnp.float32)
    v_all = value_pair.reshape(shape3).astype(jnp.float32)
    grad_all = grad_pair.reshape(shape3).astype(jnp.float32)
    factor = HD ** -0.5
    highest = lax.Precision.HIGHEST
    scores = jnp.where(permit[None], jnp.einsum("qhd,khd->hqk", q_all, k_all, precision=highest) * factor, MASKED)
    top_score = jnp.max(scores, axis=2)
    weights = jnp.exp(scores - top_score[:, :, None])
    denominator = jnp.sum(weights, axis=2)
    log_total = top_score + jnp.log(denominator)
    mixed = jnp.einsum("hqk,khd->qhd", rounded(weights), v_all, precision=highest)
    attended = (mixed / jnp.transpose(denominator)[:, :, None]).astype(jnp.bfloat16)
    delta_row = jnp.transpose(jnp.sum(grad_all * attended.astype(jnp.float32), axis=2))
    probability = jnp.exp(scores - log_total[:, :, None])
    grad_prob = jnp.einsum("qhd,khd->hqk", grad_all, v_all, precision=highest)
    dscore = rounded(probability * (grad_prob - delta_row[:, :, None]))
    grad_q = jnp.einsum("hqk,khd->qhd", dscore, k_all, precision=highest) * factor
    grad_k = jnp.einsum("hqk,qhd->khd", dscore, q_all, precision=highest) * factor
    grad_v = jnp.einsum("hqk,qhd->khd", rounded(probability), grad_all, precision=highest)
    out_shape = (2, row_count, HEADS * HD)
    return (attended.reshape(out_shape), grad_q.astype(jnp.bfloat16).reshape(out_shape),
            grad_k.astype(jnp.bfloat16).reshape(out_shape), grad_v.astype(jnp.bfloat16).reshape(out_shape))


def reference(query_heads, key_heads, value_heads, modality, doc_ids, out_weight, out_grad):
    pair_count = N_GRP // 2
    half_rows = pair_count * ROWS
    grad_parts = []
    for modal_side in range(2):
        grad_rows = out_grad[modal_side * half_rows:(modal_side + 1) * half_rows]
        grad_parts.append(lax.dot_general(grad_rows, out_weight[modal_side], (((1,), (1,)), ((), ())),
                                          preferred_element_type=jnp.float32).astype(jnp.bfloat16))
    grad_attended = jnp.concatenate(grad_parts)

    def by_pair(array):
        return jnp.swapaxes(array.reshape(2, pair_count, ROWS, array.shape[1]), 0, 1)

    def from_pair(array):
        return jnp.swapaxes(array, 0, 1).reshape(2 * half_rows, array.shape[3])

    packed = (modality[:pair_count], doc_ids[:pair_count], by_pair(query_heads), by_pair(key_heads),
              by_pair(value_heads), by_pair(grad_attended))
    attended, grad_query, grad_key, grad_value = lax.map(pair_layer, packed)
    attended = from_pair(attended)
    out_parts = []
    for modal_side in range(2):
        rows_here = attended[modal_side * half_rows:(modal_side + 1) * half_rows]
        out_parts.append(jnp.dot(rows_here, out_weight[modal_side], preferred_element_type=jnp.float32).astype(jnp.bfloat16))
    layer_output = jnp.concatenate(out_parts)
    return layer_output, from_pair(grad_query), from_pair(grad_key), from_pair(grad_value)
```

```python
import functools

import jax
import jax.numpy as jnp
from jax import lax
from jax.experimental import pallas as pl
from jax.experimental.pallas import tpu as pltpu
from jax.sharding import PartitionSpec as P

HD = 128
MASKED = -1e30
NO_KEY = 1 << 20
LAG = 2

NT = (((1,), (1,)), ((), ()))
TN = (((0,), (0,)), ((), ()))
NN = (((1,), (0,)), ((), ()))


def mul(a, b, dims):
    return lax.dot_general(a, b, dims, preferred_element_type=jnp.float32)


def swap(value, axis, by):
    devices = lax.axis_size(axis)
    return lax.ppermute(value, axis, [(i, (i + by) % devices) for i in range(devices)])


def slot_info(modal_row, doc_row, side, row_count):
    spots = jnp.arange(modal_row.shape[0], dtype=jnp.int32)
    slots = jnp.arange(row_count, dtype=jnp.int32)
    chosen = modal_row == side
    rank = jnp.sum(((spots[None, :] <= spots[:, None]) & chosen[None, :]).astype(jnp.int32), axis=1)
    doc_start = jnp.sum((doc_row[None, :] < doc_row[:, None]).astype(jnp.int32), axis=1)
    before = jnp.sum((rank[None, :] <= slots[:, None]).astype(jnp.int32), axis=1)
    slot_pos = jnp.minimum(before, modal_row.shape[0] - 1)
    slot_start = jnp.sum(jnp.where(spots[None, :] == slot_pos[:, None], doc_start[None, :], 0), axis=1)
    live = jnp.sum(chosen.astype(jnp.int32))
    return slot_pos, slot_start, live, jnp.where(slots < live, slot_pos, NO_KEY)


def step_kernel(plan, *refs):
    rows, low, tile, has_attn, has_next, has_ret, ret_base = plan
    up = rows - low
    refs = list(refs)
    n_ref = refs.pop(0)
    n_mine = n_ref[0]
    if has_attn:
        q_ref, k_ref, v_ref, g_ref, qinfo_ref, kpos_ref = (refs.pop(0) for _ in range(6))
    if has_next:
        kn_ref, vn_ref = refs.pop(0), refs.pop(0)
    msg_ref = refs.pop(0)
    if has_ret:
        own_ref = refs.pop(0)
    aliased = (2 if has_attn else 0) + (2 if has_ret else 0)
    outs = refs[len(refs) - (4 if has_attn else 0) - (2 if has_ret else 0):]
    if has_attn:
        att_ref, dq_ref, acc_ref, send_ref = (outs.pop(0) for _ in range(4))
    row_i = lax.broadcasted_iota(jnp.int32, (up, up), 0)
    col_i = lax.broadcasted_iota(jnp.int32, (up, up), 1)
    if has_ret:
        gk_ref, gv_ref = outs
        n_peer = up - n_mine
        unroll = (col_i == row_i + n_peer).astype(jnp.float32).astype(jnp.bfloat16)
        back_up = mul(unroll, msg_ref[low:rows, :], NN)
        back_low = msg_ref[ret_base:ret_base + low, :].astype(jnp.float32)
        total_low = (own_ref[0:low, :] + back_low).astype(jnp.bfloat16)
        total_up = (own_ref[low:rows, :] + back_up).astype(jnp.bfloat16)
        gk_ref[0:low, :] = total_low[:, :HD]
        gv_ref[0:low, :] = total_low[:, HD:]
        gk_ref[low:rows, :] = total_up[:, :HD]
        gv_ref[low:rows, :] = total_up[:, HD:]
    if not has_attn:
        return
    factor = HD ** (-0.5)
    keys = jnp.concatenate((k_ref[...], msg_ref[0:rows, :HD]), axis=0)
    values = jnp.concatenate((v_ref[...], msg_ref[0:rows, HD:]), axis=0)
    kpos = kpos_ref[...]
    dk = dv = None
    for first in range(0, rows, tile):
        here = slice(first, first + tile)
        q = q_ref[here, :]
        g = g_ref[here, :]
        qpos = qinfo_ref[0:1, here]
        qstart = qinfo_ref[1:2, here]
        permit = (kpos <= qpos) & (kpos >= qstart)
        scores = jnp.where(permit, mul(keys, q, NT) * factor, MASKED)
        top = jnp.max(scores, axis=0, keepdims=True)
        weights = jnp.exp(scores - top)
        inverse = 1.0 / jnp.sum(weights, axis=0, keepdims=True)
        att_t = mul(values, weights.astype(jnp.bfloat16), TN) * inverse
        att = jnp.transpose(att_t).astype(jnp.bfloat16)
        att_ref[here, :] = att
        g_t = jnp.transpose(g.astype(jnp.float32))
        delta = jnp.sum(g_t * att_t.astype(jnp.bfloat16).astype(jnp.float32), axis=0, keepdims=True)
        prob = weights * inverse
        grad_prob = mul(values, g, NT)
        dscore = (prob * (grad_prob - delta)).astype(jnp.bfloat16)
        dq_ref[here, :] = jnp.transpose(mul(keys, dscore, TN) * factor).astype(jnp.bfloat16)
        dk_part = mul(dscore, q, NN)
        dv_part = mul(prob.astype(jnp.bfloat16), g, NN)
        dk = dk_part if dk is None else dk + dk_part
        dv = dv_part if dv is None else dv + dv_part
    dk = dk * factor
    acc_ref[:, :HD] = dk[:rows]
    acc_ref[:, HD:] = dv[:rows]
    there = jnp.concatenate((dk[rows:], dv[rows:]), axis=1).astype(jnp.bfloat16)
    roll = (col_i == row_i - n_mine).astype(jnp.float32).astype(jnp.bfloat16)
    mixed = mul(roll, there[low:], NN)
    if has_next:
        own_next = jnp.concatenate((kn_ref[low:rows, :], vn_ref[low:rows, :]), axis=1)
        slot = lax.broadcasted_iota(jnp.int32, mixed.shape, 0)
        mixed = jnp.where(slot < n_mine, own_next.astype(jnp.float32), mixed)
        send_ref[0:low, :HD] = kn_ref[0:low, :]
        send_ref[0:low, HD:] = vn_ref[0:low, :]
        send_ref[rows:rows + low, :] = there[:low]
    else:
        send_ref[0:low, :] = there[:low]
    send_ref[low:rows, :] = mixed.astype(jnp.bfloat16)


def run_step(s, heads, low, n_mine, q, k, v, g, qinfo, kpos, msg, own, chains):
    rows, cols = q.shape
    has_attn = s < heads
    has_next = s + LAG < heads
    has_ret = s >= LAG
    ret_base = rows if has_attn else 0
    tile = 256 if rows % 256 == 0 else rows
    plan = (rows, low, tile, has_attn, has_next, has_ret, ret_base)

    def head_block(at):
        return pl.BlockSpec((rows, HD), lambda i: (0, at))

    def whole(array):
        return pl.BlockSpec(array.shape, lambda i: (0,) * array.ndim)

    args = [n_mine]
    specs = [pl.BlockSpec(memory_space=pltpu.SMEM)]
    if has_attn:
        args += [q, k, v, g, qinfo, kpos]
        specs += [head_block(s)] * 4 + [whole(qinfo), whole(kpos)]
    if has_next:
        args += [k, v]
        specs += [head_block(s + LAG)] * 2
    args.append(msg)
    specs.append(whole(msg))
    if has_ret:
        args.append(own)
        specs.append(whole(own))
    out_shape, out_specs, names = [], [], []
    full = jax.ShapeDtypeStruct((rows, cols), jnp.bfloat16)

    def chain_out(name, at):
        names.append(name)
        out_shape.append(full)
        out_specs.append(head_block(at))

    if has_attn:
        chain_out("att", s)
        chain_out("dq", s)
        send_rows = rows + low if has_next else rows
        names.extend(("acc", "send"))
        out_shape.append(jax.ShapeDtypeStruct((rows, 2 * HD), jnp.float32))
        out_shape.append(jax.ShapeDtypeStruct((send_rows, 2 * HD), jnp.bfloat16))
        out_specs.append(pl.BlockSpec((rows, 2 * HD), lambda i: (0, 0)))
        out_specs.append(pl.BlockSpec((send_rows, 2 * HD), lambda i: (0, 0)))
    if has_ret:
        chain_out("dk", s - LAG)
        chain_out("dv", s - LAG)
    aliases = {}
    for at, name in enumerate(names):
        if name in chains:
            aliases[len(args)] = at
            args.append(chains[name])
            specs.append(pl.BlockSpec(memory_space=pl.ANY))
    flops = 12 * rows * 2 * rows * HD if has_attn else 2 * rows * rows * HD
    results = pl.pallas_call(
        functools.partial(step_kernel, plan),
        grid=(1,),
        in_specs=specs,
        out_specs=out_specs,
        out_shape=out_shape,
        input_output_aliases=aliases,
        compiler_params=pltpu.CompilerParams(vmem_limit_bytes=48 * 1024 * 1024),
        cost_estimate=pl.CostEstimate(
            flops=flops, bytes_accessed=12 * rows * HD * 2, transcendentals=2 * rows * rows
        ),
        name="step" + str(s),
    )(*args)
    return dict(zip(names, results))


def per_device(query_heads, key_heads, value_heads, modality, doc_ids, out_weight, out_grad):
    rows, cols = query_heads.shape
    heads = cols // HD
    low = modality.shape[1] - rows
    half_grp = lax.axis_size("grp") // 2
    side = (lax.axis_index("grp") >= half_grp).astype(jnp.int32)
    exchange = functools.partial(swap, axis="grp", by=half_grp)

    def head_of(array, h):
        return array[:, h * HD:(h + 1) * HD]

    arrived = {}
    for h in range(min(LAG, heads)):
        pair = jnp.concatenate((head_of(key_heads, h), head_of(value_heads, h)), axis=1)
        arrived[h] = exchange(pair)
    pos, start, live, key_pos = slot_info(modality[0], doc_ids[0], side, rows)
    _, _, _, peer_key_pos = slot_info(modality[0], doc_ids[0], 1 - side, rows)
    qinfo = jnp.stack((pos, start))
    kpos = jnp.concatenate((key_pos, peer_key_pos))[:, None]
    n_mine = (live - low)[None]
    weight = lax.dynamic_index_in_dim(out_weight, side, 0, keepdims=False)
    grad_attended = lax.dot_general(
        out_grad, weight, NT, preferred_element_type=jnp.float32
    ).astype(jnp.bfloat16)
    chains, owns = {}, {}
    for s in range(heads + LAG):
        found = run_step(
            s, heads, low, n_mine, query_heads, key_heads, value_heads, grad_attended,
            qinfo, kpos, arrived.pop(s), owns.pop(s - LAG, None), chains,
        )
        if "send" in found:
            arrived[s + LAG] = exchange(found.pop("send"))
            owns[s] = found.pop("acc")
        chains.update(found)
        if s == heads - 1:
            partial_out = jnp.dot(chains["att"], weight, preferred_element_type=jnp.float32)
            layer_output = lax.psum_scatter(
                partial_out.astype(jnp.bfloat16), "tp", scatter_dimension=1, tiled=True
            )
    return (layer_output, chains["dq"], chains["dk"], chains["dv"])


def solution(mesh):
    placed = (
        P("grp", "tp"),
        P("grp", "tp"),
        P("grp", "tp"),
        P("grp", None),
        P("grp", None),
        P(None, "tp", None),
        P("grp", None),
    )
    return jax.shard_map(
        per_device,
        mesh=mesh,
        in_specs=placed,
        out_specs=(P("grp", "tp"), P("grp", "tp"), P("grp", "tp"), P("grp", "tp")),
        check_vma=False,
    )
```
